32 devices in a mesh: src: 8 (over z, y), tgt: 4 (over x, core).
Axes of the slice: x: 2, y: 2, z: 4, core: 2. Of those that a mesh axis runs over, the one named last changes fastest.
Arguments:
- signals: float32 [64, 98304], P(None, ('src', 'tgt')), may hold values from -6 to 6
- leaf_maps: float32 [768, 64, 128], P(('src', 'tgt')), may hold values from -0.5 to 0.5
- root_maps: float32 [768, 128, 64], P(('src', 'tgt')), may hold values from -0.75 to 0.75
- translations: float32 [8, 8, 64, 64], replicated, may hold values from -0.375 to 0.375
- source_list: int32 [8, 24, 4], replicated, may hold values from 0 to 47, as said below
- type_list: int32 [8, 24, 4], replicated, may hold values from 0 to 7
Outputs:
- focused: float32 [64, 98304], P(None, ('src', 'tgt'))
The draws below stay inside these ranges and needn't reach their ends.
Inputs may be any that keep to these rules, and one draw needn't show every extreme that they name: `source_list`: entries e < 2 name one of the device's own blocks (below 24); the other entries name one of the partner's blocks (at or above 24).
All inputs are finite; a program needn't handle non-finite values.
Results may differ from the reference program's by a relative error of at most 0.00011.
Values sent between devices are 32-bit elements; how exact they have to be, the bound alone decides.
A program may use at most 64 MiB of HBM per device.

```python
import jax
import jax.numpy as jnp
import numpy as np
from jax import lax

W = 64
R = 64
BS = 128
KB = 24
DEG = 4
NT = 8
LEVELS = 8
NB = 768
N_EL = 98304
N_SRC = 8
N_TGT = 4


def draw_source_list(key, part):
    key_base = jax.random.fold_in(key, 11)
    key_low = jax.random.fold_in(key, 12)
    key_high = jax.random.fold_in(key, 13)
    base = jax.random.randint(key_base, (LEVELS, KB, DEG), 0, KB)
    entry = jax.lax.broadcasted_iota(jnp.int32, (LEVELS, KB, DEG), 2)
    block = jax.lax.broadcasted_iota(jnp.int32, (LEVELS, KB, DEG), 1)
    low_pick = jax.random.randint(key_low, (LEVELS, 1, 1), 0, KB)
    high_pick = jax.random.randint(key_high, (LEVELS, 1, 1), 0, KB)
    base = jnp.where((block == low_pick) & (entry == 0), 0, base)
    base = jnp.where((block == high_pick) & (entry == DEG - 1), KB - 1, base)
    offset = jnp.where(entry >= DEG // 2, KB, 0)
    return (base + offset).astype(jnp.int32)


def touch_ends(entries, stream_key, least, top_value):
    shape = entries.shape
    spot = [jax.random.randint(jax.random.fold_in(stream_key, axis), (), 0, shape[axis]) for axis in range(len(shape))]
    entries = entries.at[tuple(spot)].set(least)
    longest = shape.index(max(shape))
    spot[longest] = (spot[longest] + 1) % shape[longest]
    return entries.at[tuple(spot)].set(top_value)


def levels(key, dims, cuts, smallest, top_value):
    def one(position, shards_of):
        steps = jax.random.uniform(jax.random.fold_in(jax.random.fold_in(key, 6), position), (shards_of,), jnp.float32, smallest / len(cuts), top_value / len(cuts))
        return jnp.repeat(jnp.exp(steps), dims[position] // shards_of).reshape((-1,) + (1,) * (len(dims) - position - 1))

    gain = one(*cuts[0])
    for cut in cuts[1:]:
        gain = gain * one(*cut)
    return gain


def bell_draw(rng, extent, deviation, most, split=(), kind=jnp.bfloat16):
    entries = jax.random.normal(rng, extent, jnp.float32) * deviation
    if len(split) > 0:
        entries = levels(rng, extent, split, -0.22, 0.18) * entries
    return jnp.clip(entries, min=-most, max=most).astype(kind)


def setup_inputs(seed: int = 0) -> dict:
    splits = jax.random.split(jax.random.key(seed), 7)
    signals = bell_draw(splits[0], (W, N_EL), 1.0, 6.0, ((1, 32),), jnp.float32)
    leaf_maps = bell_draw(splits[1], (NB, R, BS), BS ** -0.5, 0.5, ((0, 32),), jnp.float32)
    root_maps = bell_draw(splits[2], (NB, BS, R), R ** -0.5, 0.75, ((0, 32),), jnp.float32)
    translations = bell_draw(splits[3], (LEVELS, NT, R, R), (DEG * R) ** -0.5, 0.375, (), jnp.float32)
    source_list = draw_source_list(jax.random.fold_in(splits[6], 71), 0)
    type_list = touch_ends(jax.random.randint(splits[5], (LEVELS, KB, DEG), 0, NT), jax.random.fold_in(splits[5], 1), 0, NT - 1).astype(jnp.int32)
    return dict(signals=signals, leaf_maps=leaf_maps, root_maps=root_maps, translations=translations, source_list=source_list, type_list=type_list)


HIGH = lax.Precision.HIGHEST


def flip_along(coef, axis, count, bit):
    order = np.arange(count) ^ (1 << bit)
    return jnp.take(coef, jnp.asarray(order, dtype=jnp.int32), axis=axis)


def reference(signals, leaf_maps, root_maps, translations, source_list, type_list):
    grouped = signals.reshape(W, NB, BS)
    coef = jnp.einsum('grb,wgb->grw', leaf_maps, grouped, precision=HIGH)
    coef = coef.reshape(N_SRC, N_TGT, KB, R, W)
    src_bits = int(N_SRC).bit_length() - 1
    tgt_bits = int(N_TGT).bit_length() - 1
    for level in range(LEVELS):
        if level < LEVELS // 2:
            partner = flip_along(coef, 0, N_SRC, level % src_bits)
        else:
            partner = flip_along(coef, 1, N_TGT, (level - LEVELS // 2) % tgt_bits)
        stack = jnp.concatenate([coef, partner], axis=2)
        total = jnp.zeros((N_SRC, N_TGT, KB, R, W), jnp.float32)
        for entry in range(DEG):
            mats = translations[level][type_list[level, :, entry]]
            picked = jnp.take(stack, source_list[level, :, entry].astype(jnp.int32), axis=2)
            total = total + jnp.einsum('krs,abksw->abkrw', mats, picked, precision=HIGH)
        coef = total
    flat = coef.reshape(NB, R, W)
    focused = jnp.einsum('gbr,grw->wgb', root_maps, flat, precision=HIGH)
    return focused.reshape(W, N_EL)
```

```python
import functools

import jax
import jax.numpy as jnp
import numpy as np
from jax import lax
from jax.experimental import pallas as pl
from jax.experimental.pallas import tpu as pltpu
from jax.sharding import PartitionSpec as P

HIGH = lax.Precision.HIGHEST
MESH = pl.DeviceIdType.MESH
NT_DIMS = (((1,), (1,)), ((), ()))


def translate_shared(stack, level_src, level_types, level_table):
    mats = level_table[level_types]
    picked = stack[:, :, level_src, :]
    return jnp.einsum("kers,wnkes->wnkr", mats, picked, precision=HIGH)


def run_levels(spread, first, last, count, bits, offset, source_list, type_list, translations):
    for level in range(first, last):
        order = np.arange(count) ^ 1 << (level - offset) % bits
        partner = jnp.take(spread, jnp.asarray(order, dtype=jnp.int32), axis=1)
        stack = jnp.concatenate([spread, partner], axis=2)
        spread = translate_shared(stack, source_list[level], type_list[level], translations[level])
    return spread


def local_by_axis(signals, leaf_maps, root_maps, translations, source_list, type_list):
    blocks = leaf_maps.shape[0]
    rank = leaf_maps.shape[1]
    width = leaf_maps.shape[2]
    waves = signals.shape[0]
    grouped = signals.reshape(waves, blocks, width)
    levels = translations.shape[0]
    half = levels // 2
    src_count = lax.axis_size("src")
    tgt_count = lax.axis_size("tgt")
    src_bits = src_count.bit_length() - 1
    tgt_bits = tgt_count.bit_length() - 1
    coef = jnp.einsum("grb,wgb->wgr", leaf_maps, grouped, precision=HIGH)
    spread = lax.all_to_all(coef, "src", split_axis=0, concat_axis=1, tiled=True)
    spread = spread.reshape(waves // src_count, src_count, blocks, rank)
    spread = run_levels(
        spread, 0, half, src_count, src_bits, 0, source_list, type_list, translations
    )
    spread = spread.reshape(waves // src_count, src_count * blocks, rank)
    spread = lax.all_to_all(
        lax.all_to_all(spread, "src", split_axis=1, concat_axis=0, tiled=True),
        "tgt",
        split_axis=0,
        concat_axis=1,
        tiled=True,
    )
    spread = spread.reshape(waves // tgt_count, tgt_count, blocks, rank)
    spread = run_levels(
        spread, half, levels, tgt_count, tgt_bits, half, source_list, type_list, translations
    )
    spread = spread.reshape(waves // tgt_count, tgt_count * blocks, rank)
    coef = lax.all_to_all(spread, "tgt", split_axis=1, concat_axis=0, tiled=True)
    focused = jnp.einsum("gbr,wgr->wgb", root_maps, coef, precision=HIGH)
    return focused.reshape(waves, blocks * width)


def split(value):
    high = value.astype(jnp.bfloat16)
    low = (value - high.astype(jnp.float32)).astype(jnp.bfloat16)
    return high, low


def dot_nt(a, b):
    return lax.dot_general(a, b, NT_DIMS, preferred_element_type=jnp.float32)


def dot_nn(a, b):
    return lax.dot_general(a, b, (((1,), (0,)), ((), ())), preferred_element_type=jnp.float32)


def flip_rows(value, bit):
    rows, lanes = value.shape
    step = 1 << bit
    if step >= 8:
        parts = [value[at : at + step] for at in range(0, rows, step)]
        return jnp.concatenate([parts[i ^ 1] for i in range(len(parts))], axis=0)
    tiles = value.reshape(rows // 8, 8, lanes)
    up = pltpu.roll(tiles, step, 1)
    if step == 4:
        return up.reshape(rows, lanes)
    down = pltpu.roll(tiles, 8 - step, 1)
    place = lax.broadcasted_iota(jnp.int32, tiles.shape, 1)
    return jnp.where((place // step) % 2 == 1, up, down).reshape(rows, lanes)


def flip_scalar(value, mask, bits):
    for bit in range(bits):
        if mask >> bit & 1:
            step = 1 << bit
            value = value + step - 2 * step * ((value // step) % 2)
    return value


def slot_masks(slot, src_bits, tgt_bits):
    src_mask = sum((slot >> (src_bits - 1 - bit) & 1) << bit for bit in range(src_bits))
    return src_mask, slot >> src_bits


def fused_kernel(
    dims, sig, leaf, root_hbm, trans_hbm, slist, tlist, out,
    send_buf, recv_in, recv_out, held, table, weights, root_w, root, trans,
    send_in_sem, recv_in_sem, send_out_sem, recv_out_sem, load_sem,
):
    n_src, n_tgt, blocks, rank, width, levels, types, degree = dims
    count = n_src * n_tgt
    src_bits = n_src.bit_length() - 1
    tgt_bits = n_tgt.bit_length() - 1
    half = levels // 2
    s = lax.axis_index("src")
    t = lax.axis_index("tgt")
    me = s * n_tgt + t

    load_trans = pltpu.make_async_copy(trans_hbm, trans, load_sem.at[0])
    load_root = pltpu.make_async_copy(root_hbm, root, load_sem.at[1])
    load_trans.start()
    load_root.start()

    peers = []
    for slot in range(1, count):
        src_mask, tgt_mask = slot_masks(slot, src_bits, tgt_bits)
        peers.append((slot, flip_scalar(s, src_mask, src_bits), flip_scalar(t, tgt_mask, tgt_bits)))
    barrier = pltpu.get_barrier_semaphore()
    for slot, ps, pt in peers:
        pl.semaphore_signal(barrier, inc=1, device_id=(ps, pt), device_id_type=MESH)

    def leaf_step(k, carry):
        high, low = split(sig[:, pl.ds(pl.multiple_of(k * width, width), width)])
        map_high, map_low = split(leaf[k])
        y = dot_nt(high, map_high) + dot_nt(low, map_high) + dot_nt(high, map_low)
        pair = jnp.concatenate([y[:count], y[count:]], axis=1)
        for tile in range(count // 8):
            send_buf[pl.ds(tile * 8 * blocks + k, 8, stride=blocks), :] = pair[tile * 8 : tile * 8 + 8]
        return carry

    lax.fori_loop(0, blocks, leaf_step, 0)
    pl.semaphore_wait(barrier, count - 1)

    copies = []
    for slot, ps, pt in peers:
        copies.append(
            pltpu.make_async_remote_copy(
                src_ref=send_buf.at[pl.ds((ps * n_tgt + pt) * blocks, blocks)],
                dst_ref=recv_in.at[pl.ds(slot * blocks, blocks)],
                send_sem=send_in_sem.at[slot],
                recv_sem=recv_in_sem.at[slot],
                device_id=(ps, pt),
                device_id_type=MESH,
            )
        )
    for copy in copies:
        copy.start()
    recv_in[0:blocks, :] = send_buf[pl.ds(me * blocks, blocks), :]

    load_trans.wait()

    def weight_step(level, carry):
        for kind in range(types):
            op = trans[level, kind]
            zero = jnp.zeros_like(op)
            pair = jnp.concatenate(
                [jnp.concatenate([op, zero], axis=1), jnp.concatenate([zero, op], axis=1)], axis=0
            ).T
            high, low = split(pair)
            lanes = pl.ds(kind * 2 * rank, 2 * rank)
            weights[level, 0 : 2 * rank, lanes] = high
            weights[level, 2 * rank : 4 * rank, lanes] = high
            weights[level, 4 * rank : 6 * rank, lanes] = low
        return carry

    lax.fori_loop(0, levels, weight_step, 0)
    load_root.wait()

    def root_step(k, carry):
        high, low = split(root[k].T)
        root_w[k, 0:rank, :] = high
        root_w[k, rank : 2 * rank, :] = high
        root_w[k, 2 * rank : 3 * rank, :] = low
        return carry

    lax.fori_loop(0, blocks, root_step, 0)

    for copy in copies:
        copy.wait_recv()

    def put(k, value):
        high, low = split(value)
        rows = pl.ds(pl.multiple_of(k * count, count), count)
        held[rows, 0 : 2 * rank] = high
        held[rows, 2 * rank : 4 * rank] = low
        held[rows, 4 * rank : 6 * rank] = high

    def take_step(k, carry):
        put(
            k,
            jnp.concatenate(
                [recv_in[pl.ds(tile * 8 * blocks + k, 8, stride=blocks), :] for tile in range(count // 8)],
                axis=0,
            ),
        )
        return carry

    lax.fori_loop(0, blocks, take_step, 0)
    for copy in copies:
        copy.wait_send()

    group = 256 // count
    for level in range(levels):
        if level < half:
            bit = src_bits - 1 - level % src_bits
        else:
            bit = src_bits + (level - half) % tgt_bits

        def product_step(chunk, carry, level=level):
            rows = held[pl.ds(pl.multiple_of(chunk * group * count, group * count), group * count), :]
            for pair in range(types // 2):
                z = dot_nn(rows, weights[level, :, pair * 4 * rank : (pair + 1) * 4 * rank])
                for side in range(2):
                    table[2 * pair + side, pl.ds(chunk * group, group)] = z[
                        :, side * 2 * rank : (side + 1) * 2 * rank
                    ].reshape(group, count, 2 * rank)
            return carry

        lax.fori_loop(0, blocks // group, product_step, 0)

        def sum_step(quad, carry, level=level, bit=bit):
            for sub in range(4):
                k = quad * 4 + sub
                own = table[tlist[level, k, 0], slist[level, k, 0]]
                for e in range(1, degree // 2):
                    own = own + table[tlist[level, k, e], slist[level, k, e]]
                other = table[tlist[level, k, degree // 2], jnp.maximum(slist[level, k, degree // 2] - blocks, 0)]
                for e in range(degree // 2 + 1, degree):
                    other = other + table[tlist[level, k, e], jnp.maximum(slist[level, k, e] - blocks, 0)]
                total = own + flip_rows(other, bit)
                if level < levels - 1:
                    put(k, total)
                else:
                    for tile in range(count // 8):
                        send_buf[pl.ds(tile * 8 * blocks + k, 8, stride=blocks), :] = total[
                            tile * 8 : tile * 8 + 8
                        ]
            return carry

        lax.fori_loop(0, blocks // 4, sum_step, 0)

    returns = []
    for slot, ps, pt in peers:
        returns.append(
            pltpu.make_async_remote_copy(
                src_ref=send_buf.at[pl.ds(slot * blocks, blocks)],
                dst_ref=recv_out.at[pl.ds(me * blocks, blocks)],
                send_sem=send_out_sem.at[slot],
                recv_sem=recv_out_sem.at[slot],
                device_id=(ps, pt),
                device_id_type=MESH,
            )
        )
    for copy in returns:
        copy.start()
    recv_out[pl.ds(me * blocks, blocks), :] = send_buf[0:blocks, :]
    for copy in returns:
        copy.wait_recv()

    def focus_step(k, carry):
        pair = jnp.concatenate(
            [recv_out[pl.ds(tile * 8 * blocks + k, 8, stride=blocks), :] for tile in range(count // 8)],
            axis=0,
        )
        high, low = split(jnp.concatenate([pair[:, :rank], pair[:, rank:]], axis=0))
        y = dot_nn(jnp.concatenate([high, low, high], axis=1), root_w[k])
        out[:, pl.ds(pl.multiple_of(k * width, width), width)] = y
        return carry

    lax.fori_loop(0, blocks, focus_step, 0)
    for copy in returns:
        copy.wait_send()


def local_fused(n_src, n_tgt, signals, leaf_maps, root_maps, translations, source_list, type_list):
    blocks, rank, width = leaf_maps.shape
    levels, types = translations.shape[:2]
    degree = source_list.shape[2]
    count = n_src * n_tgt
    dims = (n_src, n_tgt, blocks, rank, width, levels, types, degree)
    vmem = pl.BlockSpec(memory_space=pltpu.VMEM)
    smem = pl.BlockSpec(memory_space=pltpu.SMEM)
    hbm = pl.BlockSpec(memory_space=pl.ANY)
    lanes = 2 * rank
    return pl.pallas_call(
        functools.partial(fused_kernel, dims),
        out_shape=jax.ShapeDtypeStruct(signals.shape, jnp.float32),
        in_specs=[vmem, vmem, hbm, hbm, smem, smem],
        out_specs=vmem,
        scratch_shapes=[
            pltpu.VMEM((count * blocks, lanes), jnp.float32),
            pltpu.VMEM((count * blocks, lanes), jnp.float32),
            pltpu.VMEM((count * blocks, lanes), jnp.float32),
            pltpu.VMEM((blocks * count, 3 * lanes), jnp.bfloat16),
            pltpu.VMEM((types, blocks, count, lanes), jnp.float32),
            pltpu.VMEM((levels, 3 * lanes, types * lanes), jnp.bfloat16),
            pltpu.VMEM((blocks, 3 * rank, width), jnp.bfloat16),
            pltpu.VMEM(root_maps.shape, jnp.float32),
            pltpu.VMEM(translations.shape, jnp.float32),
            pltpu.SemaphoreType.DMA((count,)),
            pltpu.SemaphoreType.DMA((count,)),
            pltpu.SemaphoreType.DMA((count,)),
            pltpu.SemaphoreType.DMA((count,)),
            pltpu.SemaphoreType.DMA((2,)),
        ],
        compiler_params=pltpu.CompilerParams(
            collective_id=0, has_side_effects=True, vmem_limit_bytes=40 * 1024 * 1024
        ),
        cost_estimate=pl.CostEstimate(flops=10**9, bytes_accessed=5 * 10**6, transcendentals=0),
    )(signals, leaf_maps, root_maps, translations, source_list, type_list)


def is_power(value):
    return value > 1 and value & (value - 1) == 0


def solution(mesh):
    placed = (
        P(None, ("src", "tgt")),
        P(("src", "tgt"), None, None),
        P(("src", "tgt"), None, None),
        P(),
        P(),
        P(),
    )
    n_src, n_tgt = mesh.shape["src"], mesh.shape["tgt"]

    def local(signals, leaf_maps, *rest):
        blocks, rank, width = leaf_maps.shape
        fits = (
            signals.shape[0] == 2 * n_src * n_tgt
            and is_power(n_src)
            and is_power(n_tgt)
            and 256 % (n_src * n_tgt) == 0
            and blocks % 8 == 0
            and blocks % (256 // (n_src * n_tgt)) == 0
            and rank == 64
            and width == 128
        )
        if fits:
            return local_fused(n_src, n_tgt, signals, leaf_maps, *rest)
        return local_by_axis(signals, leaf_maps, *rest)

    return jax.shard_map(
        local, mesh=mesh, in_specs=placed, out_specs=P(None, ("src", "tgt")), check_vma=False
    )
```

```python
import functools

import jax
import jax.numpy as jnp
import numpy as np
from jax import lax
from jax.experimental import pallas as pl
from jax.experimental.pallas import tpu as pltpu
from jax.sharding import PartitionSpec as P

HIGH = lax.Precision.HIGHEST
MESH = pl.DeviceIdType.MESH
NT_DIMS = (((1,), (1,)), ((), ()))


def translate_shared(stack, level_src, level_types, level_table):
    mats = level_table[level_types]
    picked = stack[:, :, level_src, :]
    return jnp.einsum("kers,wnkes->wnkr", mats, picked, precision=HIGH)


def run_levels(spread, first, last, count, bits, offset, source_list, type_list, translations):
    for level in range(first, last):
        order = np.arange(count) ^ 1 << (level - offset) % bits
        partner = jnp.take(spread, jnp.asarray(order, dtype=jnp.int32), axis=1)
        stack = jnp.concatenate([spread, partner], axis=2)
        spread = translate_shared(stack, source_list[level], type_list[level], translations[level])
    return spread


def local_by_axis(signals, leaf_maps, root_maps, translations, source_list, type_list):
    blocks = leaf_maps.shape[0]
    rank = leaf_maps.shape[1]
    width = leaf_maps.shape[2]
    waves = signals.shape[0]
    grouped = signals.reshape(waves, blocks, width)
    levels = translations.shape[0]
    half = levels // 2
    src_count = lax.axis_size("src")
    tgt_count = lax.axis_size("tgt")
    src_bits = src_count.bit_length() - 1
    tgt_bits = tgt_count.bit_length() - 1
    coef = jnp.einsum("grb,wgb->wgr", leaf_maps, grouped, precision=HIGH)
    spread = lax.all_to_all(coef, "src", split_axis=0, concat_axis=1, tiled=True)
    spread = spread.reshape(waves // src_count, src_count, blocks, rank)
    spread = run_levels(
        spread, 0, half, src_count, src_bits, 0, source_list, type_list, translations
    )
    spread = spread.reshape(waves // src_count, src_count * blocks, rank)
    spread = lax.all_to_all(
        lax.all_to_all(spread, "src", split_axis=1, concat_axis=0, tiled=True),
        "tgt",
        split_axis=0,
        concat_axis=1,
        tiled=True,
    )
    spread = spread.reshape(waves // tgt_count, tgt_count, blocks, rank)
    spread = run_levels(
        spread, half, levels, tgt_count, tgt_bits, half, source_list, type_list, translations
    )
    spread = spread.reshape(waves // tgt_count, tgt_count * blocks, rank)
    coef = lax.all_to_all(spread, "tgt", split_axis=1, concat_axis=0, tiled=True)
    focused = jnp.einsum("gbr,wgr->wgb", root_maps, coef, precision=HIGH)
    return focused.reshape(waves, blocks * width)


def split(value):
    high = value.astype(jnp.bfloat16)
    low = (value - high.astype(jnp.float32)).astype(jnp.bfloat16)
    return high, low


def dot_nt(a, b):
    return lax.dot_general(a, b, NT_DIMS, preferred_element_type=jnp.float32)


def dot_nn(a, b):
    return lax.dot_general(a, b, (((1,), (0,)), ((), ())), preferred_element_type=jnp.float32)


def flip_rows(value, bit):
    rows, lanes = value.shape
    step = 1 << bit
    if step >= 8:
        parts = [value[at : at + step] for at in range(0, rows, step)]
        return jnp.concatenate([parts[i ^ 1] for i in range(len(parts))], axis=0)
    tiles = value.reshape(rows // 8, 8, lanes)
    up = pltpu.roll(tiles, step, 1)
    if step == 4:
        return up.reshape(rows, lanes)
    down = pltpu.roll(tiles, 8 - step, 1)
    place = lax.broadcasted_iota(jnp.int32, tiles.shape, 1)
    return jnp.where((place // step) % 2 == 1, up, down).reshape(rows, lanes)


def flip_scalar(value, mask, bits):
    for bit in range(bits):
        if mask >> bit & 1:
            step = 1 << bit
            value = value + step - 2 * step * ((value // step) % 2)
    return value


def slot_masks(slot, src_bits, tgt_bits):
    src_mask = sum((slot >> (src_bits - 1 - bit) & 1) << bit for bit in range(src_bits))
    return src_mask, slot >> src_bits


def fused_kernel(
    dims, sig_hbm, leaf_hbm, root_hbm, trans_hbm, slist, tlist, out,
    send_buf, recv_in, recv_out, held, table_a, table_b, weights, root_w, sig, leaf, root, trans,
    send_in_sem, recv_in_sem, send_out_sem, recv_out_sem, load_sem,
):
    n_src, n_tgt, blocks, rank, width, levels, types, degree = dims
    count = n_src * n_tgt
    src_bits = n_src.bit_length() - 1
    tgt_bits = n_tgt.bit_length() - 1
    half = levels // 2
    group = 256 // count
    chunks = blocks // group
    tables = (table_a, table_b)
    s = lax.axis_index("src")
    t = lax.axis_index("tgt")
    me = s * n_tgt + t

    loads = [
        pltpu.make_async_copy(source, target, load_sem.at[i])
        for i, (source, target) in enumerate(
            ((sig_hbm, sig), (leaf_hbm, leaf), (trans_hbm, trans), (root_hbm, root))
        )
    ]
    for load in loads:
        load.start()

    peers = []
    for slot in range(1, count):
        src_mask, tgt_mask = slot_masks(slot, src_bits, tgt_bits)
        peers.append((slot, flip_scalar(s, src_mask, src_bits), flip_scalar(t, tgt_mask, tgt_bits)))
    barrier = pltpu.get_barrier_semaphore()
    for slot, ps, pt in peers:
        pl.semaphore_signal(barrier, inc=1, device_id=(ps, pt), device_id_type=MESH)

    def spread_rows(ref, k, value):
        for tile in range(count // 8):
            ref[pl.ds(tile * 8 * blocks + k, 8, stride=blocks), :] = value[tile * 8 : tile * 8 + 8]

    def gather_rows(ref, k):
        return jnp.concatenate(
            [ref[pl.ds(tile * 8 * blocks + k, 8, stride=blocks), :] for tile in range(count // 8)],
            axis=0,
        )

    loads[0].wait()
    loads[1].wait()
    copies = []
    for chunk in range(chunks):
        for k in range(chunk * group, (chunk + 1) * group):
            high, low = split(sig[:, k * width : (k + 1) * width])
            map_high, map_low = split(leaf[k])
            y = dot_nt(
                jnp.concatenate([high, low, high], axis=1),
                jnp.concatenate([map_high, map_high, map_low], axis=1),
            )
            spread_rows(send_buf, k, jnp.concatenate([y[:count], y[count:]], axis=1))
        if chunk == 0:
            pl.semaphore_wait(barrier, count - 1)
        started = []
        for slot, ps, pt in reversed(peers):
            copy = pltpu.make_async_remote_copy(
                src_ref=send_buf.at[pl.ds((ps * n_tgt + pt) * blocks + chunk * group, group)],
                dst_ref=recv_in.at[pl.ds(slot * blocks + chunk * group, group)],
                send_sem=send_in_sem.at[chunk, slot],
                recv_sem=recv_in_sem.at[chunk, slot],
                device_id=(ps, pt),
                device_id_type=MESH,
            )
            copy.start()
            started.append(copy)
        copies.append(started)
    recv_in[0:blocks, :] = send_buf[pl.ds(me * blocks, blocks), :]

    loads[2].wait()

    def weight_step(level, carry):
        for kind in range(types):
            op = trans[level, kind]
            zero = jnp.zeros_like(op)
            pair = jnp.concatenate(
                [jnp.concatenate([op, zero], axis=1), jnp.concatenate([zero, op], axis=1)], axis=0
            ).T
            high, low = split(pair)
            lanes = pl.ds(kind * 2 * rank, 2 * rank)
            weights[level, 0 : 2 * rank, lanes] = high
            weights[level, 2 * rank : 4 * rank, lanes] = high
            weights[level, 4 * rank : 6 * rank, lanes] = low
        return carry

    lax.fori_loop(0, levels, weight_step, 0)
    loads[3].wait()

    def root_step(k, carry):
        high, low = split(root[k])
        root_w[k, 0:rank, :] = high
        root_w[k, rank : 2 * rank, :] = high
        root_w[k, 2 * rank : 3 * rank, :] = low
        return carry

    lax.fori_loop(0, blocks, root_step, 0)

    def put(k, value):
        high, low = split(value)
        rows = slice(k * count, (k + 1) * count)
        held[rows, 0 : 2 * rank] = high
        held[rows, 2 * rank : 4 * rank] = low
        held[rows, 4 * rank : 6 * rank] = high

    def multiply(level, chunk):
        rows = held[chunk * group * count : (chunk + 1) * group * count, :]
        for pair in range(types // 2):
            z = dot_nn(rows, weights[level, :, pair * 4 * rank : (pair + 1) * 4 * rank])
            for side in range(2):
                tables[level % 2][2 * pair + side, chunk * group : (chunk + 1) * group] = z[
                    :, side * 2 * rank : (side + 1) * 2 * rank
                ].reshape(group, count, 2 * rank)

    def add_up(level, k):
        if level < half:
            bit = src_bits - 1 - level % src_bits
        else:
            bit = src_bits + (level - half) % tgt_bits
        table = tables[level % 2]
        own = other = None
        for e in range(degree):
            source = slist[level, e, k]
            if e < degree // 2:
                part = table[tlist[level, e, k], source]
                own = part if own is None else own + part
            else:
                part = table[tlist[level, e, k], jnp.maximum(source - blocks, 0)]
                other = part if other is None else other + part
        return own + flip_rows(other, bit)

    for chunk in range(chunks):
        for copy in copies[chunk]:
            copy.wait_recv()
        for k in range(chunk * group, (chunk + 1) * group):
            put(k, gather_rows(recv_in, k))
        multiply(0, chunk)
    for started in copies:
        for copy in started:
            copy.wait_send()

    for level in range(levels - 1):
        for chunk in range(chunks):
            for k in range(chunk * group, (chunk + 1) * group):
                put(k, add_up(level, k))
            multiply(level + 1, chunk)

    returns = []
    for chunk in range(chunks):
        for k in range(chunk * group, (chunk + 1) * group):
            spread_rows(send_buf, k, add_up(levels - 1, k))
        started = []
        for slot, ps, pt in reversed(peers):
            copy = pltpu.make_async_remote_copy(
                src_ref=send_buf.at[pl.ds(slot * blocks + chunk * group, group)],
                dst_ref=recv_out.at[pl.ds(me * blocks + chunk * group, group)],
                send_sem=send_out_sem.at[chunk, slot],
                recv_sem=recv_out_sem.at[chunk, slot],
                device_id=(ps, pt),
                device_id_type=MESH,
            )
            copy.start()
            started.append(copy)
        returns.append(started)
    recv_out[pl.ds(me * blocks, blocks), :] = send_buf[0:blocks, :]

    for chunk in range(chunks):
        for copy in returns[chunk]:
            copy.wait_recv()
        for k in range(chunk * group, (chunk + 1) * group):
            pair = gather_rows(recv_out, k)
            high, low = split(jnp.concatenate([pair[:, :rank], pair[:, rank:]], axis=0))
            y = dot_nn(jnp.concatenate([high, low, high], axis=1), root_w[k])
            out[:, k * width : (k + 1) * width] = y
    for started in returns:
        for copy in started:
            copy.wait_send()


def local_fused(n_src, n_tgt, signals, leaf_maps, root_maps, translations, source_list, type_list):
    blocks, rank, width = leaf_maps.shape
    levels, types = translations.shape[:2]
    degree = source_list.shape[2]
    count = n_src * n_tgt
    dims = (n_src, n_tgt, blocks, rank, width, levels, types, degree)
    vmem = pl.BlockSpec(memory_space=pltpu.VMEM)
    smem = pl.BlockSpec(memory_space=pltpu.SMEM)
    hbm = pl.BlockSpec(memory_space=pl.ANY)
    lanes = 2 * rank
    chunks = blocks // (256 // count)
    return pl.pallas_call(
        functools.partial(fused_kernel, dims),
        out_shape=jax.ShapeDtypeStruct(signals.shape, jnp.float32),
        in_specs=[hbm, hbm, hbm, hbm, smem, smem],
        out_specs=vmem,
        scratch_shapes=[
            pltpu.VMEM((count * blocks, lanes), jnp.float32),
            pltpu.VMEM((count * blocks, lanes), jnp.float32),
            pltpu.VMEM((count * blocks, lanes), jnp.float32),
            pltpu.VMEM((blocks * count, 3 * lanes), jnp.bfloat16),
            pltpu.VMEM((types, blocks, count, lanes), jnp.float32),
            pltpu.VMEM((types, blocks, count, lanes), jnp.float32),
            pltpu.VMEM((levels, 3 * lanes, types * lanes), jnp.bfloat16),
            pltpu.VMEM((blocks, 3 * rank, width), jnp.bfloat16),
            pltpu.VMEM(signals.shape, jnp.float32),
            pltpu.VMEM(leaf_maps.shape, jnp.float32),
            pltpu.VMEM((blocks, rank, width), jnp.float32),
            pltpu.VMEM(translations.shape, jnp.float32),
            pltpu.SemaphoreType.DMA((chunks, count)),
            pltpu.SemaphoreType.DMA((chunks, count)),
            pltpu.SemaphoreType.DMA((chunks, count)),
            pltpu.SemaphoreType.DMA((chunks, count)),
            pltpu.SemaphoreType.DMA((4,)),
        ],
        compiler_params=pltpu.CompilerParams(
            collective_id=0, has_side_effects=True, vmem_limit_bytes=58 * 1024 * 1024
        ),
        cost_estimate=pl.CostEstimate(flops=10**9, bytes_accessed=5 * 10**6, transcendentals=0),
    )(
        signals,
        leaf_maps,
        jnp.swapaxes(root_maps, 1, 2),
        translations,
        jnp.swapaxes(source_list, 1, 2),
        jnp.swapaxes(type_list, 1, 2),
    )


def is_power(value):
    return value > 1 and value & (value - 1) == 0


def solution(mesh):
    placed = (
        P(None, ("src", "tgt")),
        P(("src", "tgt"), None, None),
        P(("src", "tgt"), None, None),
        P(),
        P(),
        P(),
    )
    n_src, n_tgt = mesh.shape["src"], mesh.shape["tgt"]

    def local(signals, leaf_maps, *rest):
        blocks, rank, width = leaf_maps.shape
        fits = (
            signals.shape[0] == 2 * n_src * n_tgt
            and is_power(n_src)
            and is_power(n_tgt)
            and 256 % (n_src * n_tgt) == 0
            and blocks % 8 == 0
            and blocks % (256 // (n_src * n_tgt)) == 0
            and rank == 64
            and width == 128
        )
        if fits:
            return local_fused(n_src, n_tgt, signals, leaf_maps, *rest)
        return local_by_axis(signals, leaf_maps, *rest)

    return jax.shard_map(
        local, mesh=mesh, in_specs=placed, out_specs=P(None, ("src", "tgt")), check_vma=False
    )
```

```python
import functools

import jax
import jax.numpy as jnp
import numpy as np
from jax import lax
from jax.experimental import pallas as pl
from jax.experimental.pallas import tpu as pltpu
from jax.sharding import PartitionSpec as P

HIGH = lax.Precision.HIGHEST
MESH = pl.DeviceIdType.MESH
NT_DIMS = (((1,), (1,)), ((), ()))


def translate_shared(stack, level_src, level_types, level_table):
    mats = level_table[level_types]
    picked = stack[:, :, level_src, :]
    return jnp.einsum("kers,wnkes->wnkr", mats, picked, precision=HIGH)


def run_levels(spread, first, last, count, bits, offset, source_list, type_list, translations):
    for level in range(first, last):
        order = np.arange(count) ^ 1 << (level - offset) % bits
        partner = jnp.take(spread, jnp.asarray(order, dtype=jnp.int32), axis=1)
        stack = jnp.concatenate([spread, partner], axis=2)
        spread = translate_shared(stack, source_list[level], type_list[level], translations[level])
    return spread


def local_by_axis(signals, leaf_maps, root_maps, translations, source_list, type_list):
    blocks = leaf_maps.shape[0]
    rank = leaf_maps.shape[1]
    width = leaf_maps.shape[2]
    waves = signals.shape[0]
    grouped = signals.reshape(waves, blocks, width)
    levels = translations.shape[0]
    half = levels // 2
    src_count = lax.axis_size("src")
    tgt_count = lax.axis_size("tgt")
    src_bits = src_count.bit_length() - 1
    tgt_bits = tgt_count.bit_length() - 1
    coef = jnp.einsum("grb,wgb->wgr", leaf_maps, grouped, precision=HIGH)
    spread = lax.all_to_all(coef, "src", split_axis=0, concat_axis=1, tiled=True)
    spread = spread.reshape(waves // src_count, src_count, blocks, rank)
    spread = run_levels(
        spread, 0, half, src_count, src_bits, 0, source_list, type_list, translations
    )
    spread = spread.reshape(waves // src_count, src_count * blocks, rank)
    spread = lax.all_to_all(
        lax.all_to_all(spread, "src", split_axis=1, concat_axis=0, tiled=True),
        "tgt",
        split_axis=0,
        concat_axis=1,
        tiled=True,
    )
    spread = spread.reshape(waves // tgt_count, tgt_count, blocks, rank)
    spread = run_levels(
        spread, half, levels, tgt_count, tgt_bits, half, source_list, type_list, translations
    )
    spread = spread.reshape(waves // tgt_count, tgt_count * blocks, rank)
    coef = lax.all_to_all(spread, "tgt", split_axis=1, concat_axis=0, tiled=True)
    focused = jnp.einsum("gbr,wgr->wgb", root_maps, coef, precision=HIGH)
    return focused.reshape(waves, blocks * width)


def split(value):
    high = value.astype(jnp.bfloat16)
    low = (value - high.astype(jnp.float32)).astype(jnp.bfloat16)
    return high, low


def dot_nt(a, b):
    return lax.dot_general(a, b, NT_DIMS, preferred_element_type=jnp.float32)


def dot_nn(a, b):
    return lax.dot_general(a, b, (((1,), (0,)), ((), ())), preferred_element_type=jnp.float32)


def flip_rows(value, bit):
    rows, lanes = value.shape
    step = 1 << bit
    if step >= 8:
        parts = [value[at : at + step] for at in range(0, rows, step)]
        return jnp.concatenate([parts[i ^ 1] for i in range(len(parts))], axis=0)
    tiles = value.reshape(rows // 8, 8, lanes)
    up = pltpu.roll(tiles, step, 1)
    if step == 4:
        return up.reshape(rows, lanes)
    down = pltpu.roll(tiles, 8 - step, 1)
    place = lax.broadcasted_iota(jnp.int32, tiles.shape, 1)
    return jnp.where((place // step) % 2 == 1, up, down).reshape(rows, lanes)


def flip_scalar(value, mask, bits):
    for bit in range(bits):
        if mask >> bit & 1:
            step = 1 << bit
            value = value + step - 2 * step * ((value // step) % 2)
    return value


def slot_masks(slot, src_bits, tgt_bits):
    src_mask = sum((slot >> (src_bits - 1 - bit) & 1) << bit for bit in range(src_bits))
    return src_mask, slot >> src_bits


def fused_kernel(
    dims, sig_hbm, leaf_hbm, root_hbm, trans_hbm, slist, tlist, out,
    send_buf, recv_in, recv_out, held, table_a, table_b, weights, root_w, sig, leaf, root, trans,
    send_in_sem, recv_in_sem, send_out_sem, recv_out_sem, load_sem,
):
    n_src, n_tgt, blocks, rank, width, levels, types, degree = dims
    count = n_src * n_tgt
    src_bits = n_src.bit_length() - 1
    tgt_bits = n_tgt.bit_length() - 1
    half = levels // 2
    group = 256 // count
    chunks = blocks // group
    tables = (table_a, table_b)
    s = lax.axis_index("src")
    t = lax.axis_index("tgt")
    me = s * n_tgt + t

    loads = [
        pltpu.make_async_copy(source, target, load_sem.at[i])
        for i, (source, target) in enumerate(
            ((sig_hbm, sig), (leaf_hbm, leaf), (trans_hbm, trans), (root_hbm, root))
        )
    ]
    for load in loads:
        load.start()

    peers = []
    for slot in range(1, count):
        src_mask, tgt_mask = slot_masks(slot, src_bits, tgt_bits)
        peers.append((slot, flip_scalar(s, src_mask, src_bits), flip_scalar(t, tgt_mask, tgt_bits)))
    barrier = pltpu.get_barrier_semaphore()
    for slot, ps, pt in peers:
        pl.semaphore_signal(barrier, inc=1, device_id=(ps, pt), device_id_type=MESH)

    def spread_rows(ref, k, value):
        for tile in range(count // 8):
            ref[pl.ds(tile * 8 * blocks + k, 8, stride=blocks), :] = value[tile * 8 : tile * 8 + 8]

    def gather_rows(ref, k):
        return jnp.concatenate(
            [ref[pl.ds(tile * 8 * blocks + k, 8, stride=blocks), :] for tile in range(count // 8)],
            axis=0,
        )

    def wait_bytes(ref, rows, sem):
        part = ref.at[pl.ds(0, rows)]
        pltpu.make_async_copy(part, part, sem).wait()

    loads[0].wait()
    loads[1].wait()
    for chunk in range(chunks):
        for k in range(chunk * group, (chunk + 1) * group):
            high, low = split(sig[:, k * width : (k + 1) * width])
            map_high, map_low = split(leaf[k])
            y = dot_nt(
                jnp.concatenate([high, low, high], axis=1),
                jnp.concatenate([map_high, map_high, map_low], axis=1),
            )
            spread_rows(send_buf, k, jnp.concatenate([y[:count], y[count:]], axis=1))
        if chunk == 0:
            pl.semaphore_wait(barrier, count - 1)
        for slot, ps, pt in reversed(peers):
            copy = pltpu.make_async_remote_copy(
                src_ref=send_buf.at[pl.ds((ps * n_tgt + pt) * blocks + chunk * group, group)],
                dst_ref=recv_in.at[pl.ds(slot * blocks + chunk * group, group)],
                send_sem=send_in_sem.at[0],
                recv_sem=recv_in_sem.at[chunk],
                device_id=(ps, pt),
                device_id_type=MESH,
            )
            copy.start()
    recv_in[0:blocks, :] = send_buf[pl.ds(me * blocks, blocks), :]

    loads[2].wait()

    def weight_step(level, carry):
        for kind in range(types):
            op = trans[level, kind]
            zero = jnp.zeros_like(op)
            pair = jnp.concatenate(
                [jnp.concatenate([op, zero], axis=1), jnp.concatenate([zero, op], axis=1)], axis=0
            ).T
            high, low = split(pair)
            lanes = pl.ds(kind * 2 * rank, 2 * rank)
            weights[level, 0 : 2 * rank, lanes] = high
            weights[level, 2 * rank : 4 * rank, lanes] = high
            weights[level, 4 * rank : 6 * rank, lanes] = low
        return carry

    lax.fori_loop(0, levels, weight_step, 0)
    loads[3].wait()

    def root_step(k, carry):
        high, low = split(root[k])
        root_w[k, 0:rank, :] = high
        root_w[k, rank : 2 * rank, :] = high
        root_w[k, 2 * rank : 3 * rank, :] = low
        return carry

    lax.fori_loop(0, blocks, root_step, 0)

    def put(k, value):
        high, low = split(value)
        rows = slice(k * count, (k + 1) * count)
        held[rows, 0 : 2 * rank] = high
        held[rows, 2 * rank : 4 * rank] = low
        held[rows, 4 * rank : 6 * rank] = high

    def multiply(level, chunk):
        rows = held[chunk * group * count : (chunk + 1) * group * count, :]
        for pair in range(types // 2):
            z = dot_nn(rows, weights[level, :, pair * 4 * rank : (pair + 1) * 4 * rank])
            for side in range(2):
                tables[level % 2][2 * pair + side, chunk * group : (chunk + 1) * group] = z[
                    :, side * 2 * rank : (side + 1) * 2 * rank
                ].reshape(group, count, 2 * rank)

    def add_up(level, k):
        if level < half:
            bit = src_bits - 1 - level % src_bits
        else:
            bit = src_bits + (level - half) % tgt_bits
        table = tables[level % 2]
        own = other = None
        for e in range(degree):
            source = slist[level, e, k]
            if e < degree // 2:
                part = table[tlist[level, e, k], source]
                own = part if own is None else own + part
            else:
                part = table[tlist[level, e, k], jnp.maximum(source - blocks, 0)]
                other = part if other is None else other + part
        return own + flip_rows(other, bit)

    for chunk in range(chunks):
        wait_bytes(recv_in, (count - 1) * group, recv_in_sem.at[chunk])
        for k in range(chunk * group, (chunk + 1) * group):
            put(k, gather_rows(recv_in, k))
        multiply(0, chunk)
    wait_bytes(send_buf, (count - 1) * blocks, send_in_sem.at[0])

    for level in range(levels - 1):
        for chunk in range(chunks):
            for k in range(chunk * group, (chunk + 1) * group):
                put(k, add_up(level, k))
            multiply(level + 1, chunk)

    for chunk in range(chunks):
        for k in range(chunk * group, (chunk + 1) * group):
            spread_rows(send_buf, k, add_up(levels - 1, k))
        for slot, ps, pt in reversed(peers):
            copy = pltpu.make_async_remote_copy(
                src_ref=send_buf.at[pl.ds(slot * blocks + chunk * group, group)],
                dst_ref=recv_out.at[pl.ds(me * blocks + chunk * group, group)],
                send_sem=send_out_sem.at[0],
                recv_sem=recv_out_sem.at[chunk],
                device_id=(ps, pt),
                device_id_type=MESH,
            )
            copy.start()
    recv_out[pl.ds(me * blocks, blocks), :] = send_buf[0:blocks, :]

    for chunk in range(chunks):
        wait_bytes(recv_out, (count - 1) * group, recv_out_sem.at[chunk])
        for k in range(chunk * group, (chunk + 1) * group):
            pair = gather_rows(recv_out, k)
            high, low = split(jnp.concatenate([pair[:, :rank], pair[:, rank:]], axis=0))
            y = dot_nn(jnp.concatenate([high, low, high], axis=1), root_w[k])
            out[:, k * width : (k + 1) * width] = y
    wait_bytes(send_buf, (count - 1) * blocks, send_out_sem.at[0])


def local_fused(n_src, n_tgt, signals, leaf_maps, root_maps, translations, source_list, type_list):
    blocks, rank, width = leaf_maps.shape
    levels, types = translations.shape[:2]
    degree = source_list.shape[2]
    count = n_src * n_tgt
    dims = (n_src, n_tgt, blocks, rank, width, levels, types, degree)
    vmem = pl.BlockSpec(memory_space=pltpu.VMEM)
    smem = pl.BlockSpec(memory_space=pltpu.SMEM)
    hbm = pl.BlockSpec(memory_space=pl.ANY)
    lanes = 2 * rank
    chunks = blocks // (256 // count)
    return pl.pallas_call(
        functools.partial(fused_kernel, dims),
        out_shape=jax.ShapeDtypeStruct(signals.shape, jnp.float32),
        in_specs=[hbm, hbm, hbm, hbm, smem, smem],
        out_specs=vmem,
        scratch_shapes=[
            pltpu.VMEM((count * blocks, lanes), jnp.float32),
            pltpu.VMEM((count * blocks, lanes), jnp.float32),
            pltpu.VMEM((count * blocks, lanes), jnp.float32),
            pltpu.VMEM((blocks * count, 3 * lanes), jnp.bfloat16),
            pltpu.VMEM((types, blocks, count, lanes), jnp.float32),
            pltpu.VMEM((types, blocks, count, lanes), jnp.float32),
            pltpu.VMEM((levels, 3 * lanes, types * lanes), jnp.bfloat16),
            pltpu.VMEM((blocks, 3 * rank, width), jnp.bfloat16),
            pltpu.VMEM(signals.shape, jnp.float32),
            pltpu.VMEM(leaf_maps.shape, jnp.float32),
            pltpu.VMEM((blocks, rank, width), jnp.float32),
            pltpu.VMEM(translations.shape, jnp.float32),
            pltpu.SemaphoreType.DMA((1,)),
            pltpu.SemaphoreType.DMA((chunks,)),
            pltpu.SemaphoreType.DMA((1,)),
            pltpu.SemaphoreType.DMA((chunks,)),
            pltpu.SemaphoreType.DMA((4,)),
        ],
        compiler_params=pltpu.CompilerParams(
            collective_id=0, has_side_effects=True, vmem_limit_bytes=58 * 1024 * 1024
        ),
        cost_estimate=pl.CostEstimate(flops=10**9, bytes_accessed=5 * 10**6, transcendentals=0),
    )(
        signals,
        leaf_maps,
        jnp.swapaxes(root_maps, 1, 2),
        translations,
        jnp.swapaxes(source_list, 1, 2),
        jnp.swapaxes(type_list, 1, 2),
    )


def is_power(value):
    return value > 1 and value & (value - 1) == 0


def solution(mesh):
    placed = (
        P(None, ("src", "tgt")),
        P(("src", "tgt"), None, None),
        P(("src", "tgt"), None, None),
        P(),
        P(),
        P(),
    )
    n_src, n_tgt = mesh.shape["src"], mesh.shape["tgt"]

    def local(signals, leaf_maps, *rest):
        blocks, rank, width = leaf_maps.shape
        fits = (
            signals.shape[0] == 2 * n_src * n_tgt
            and is_power(n_src)
            and is_power(n_tgt)
            and 256 % (n_src * n_tgt) == 0
            and blocks % 8 == 0
            and blocks % (256 // (n_src * n_tgt)) == 0
            and rank == 64
            and width == 128
        )
        if fits:
            return local_fused(n_src, n_tgt, signals, leaf_maps, *rest)
        return local_by_axis(signals, leaf_maps, *rest)

    return jax.shard_map(
        local, mesh=mesh, in_specs=placed, out_specs=P(None, ("src", "tgt")), check_vma=False
    )
```

```python
import functools

import jax
import jax.numpy as jnp
import numpy as np
from jax import lax
from jax.experimental import pallas as pl
from jax.experimental.pallas import tpu as pltpu
from jax.sharding import PartitionSpec as P

HIGH = lax.Precision.HIGHEST
MESH = pl.DeviceIdType.MESH
NT_DIMS = (((1,), (1,)), ((), ()))


def translate_shared(stack, level_src, level_types, level_table):
    mats = level_table[level_types]
    picked = stack[:, :, level_src, :]
    return jnp.einsum("kers,wnkes->wnkr", mats, picked, precision=HIGH)


def run_levels(spread, first, last, count, bits, offset, source_list, type_list, translations):
    for level in range(first, last):
        order = np.arange(count) ^ 1 << (level - offset) % bits
        partner = jnp.take(spread, jnp.asarray(order, dtype=jnp.int32), axis=1)
        stack = jnp.concatenate([spread, partner], axis=2)
        spread = translate_shared(stack, source_list[level], type_list[level], translations[level])
    return spread


def local_by_axis(signals, leaf_maps, root_maps, translations, source_list, type_list):
    blocks = leaf_maps.shape[0]
    rank = leaf_maps.shape[1]
    width = leaf_maps.shape[2]
    waves = signals.shape[0]
    grouped = signals.reshape(waves, blocks, width)
    levels = translations.shape[0]
    half = levels // 2
    src_count = lax.axis_size("src")
    tgt_count = lax.axis_size("tgt")
    src_bits = src_count.bit_length() - 1
    tgt_bits = tgt_count.bit_length() - 1
    coef = jnp.einsum("grb,wgb->wgr", leaf_maps, grouped, precision=HIGH)
    spread = lax.all_to_all(coef, "src", split_axis=0, concat_axis=1, tiled=True)
    spread = spread.reshape(waves // src_count, src_count, blocks, rank)
    spread = run_levels(
        spread, 0, half, src_count, src_bits, 0, source_list, type_list, translations
    )
    spread = spread.reshape(waves // src_count, src_count * blocks, rank)
    spread = lax.all_to_all(
        lax.all_to_all(spread, "src", split_axis=1, concat_axis=0, tiled=True),
        "tgt",
        split_axis=0,
        concat_axis=1,
        tiled=True,
    )
    spread = spread.reshape(waves // tgt_count, tgt_count, blocks, rank)
    spread = run_levels(
        spread, half, levels, tgt_count, tgt_bits, half, source_list, type_list, translations
    )
    spread = spread.reshape(waves // tgt_count, tgt_count * blocks, rank)
    coef = lax.all_to_all(spread, "tgt", split_axis=1, concat_axis=0, tiled=True)
    focused = jnp.einsum("gbr,wgr->wgb", root_maps, coef, precision=HIGH)
    return focused.reshape(waves, blocks * width)


def split(value):
    high = value.astype(jnp.bfloat16)
    low = (value - high.astype(jnp.float32)).astype(jnp.bfloat16)
    return high, low


def dot_nt(a, b):
    return lax.dot_general(a, b, NT_DIMS, preferred_element_type=jnp.float32)


def dot_nn(a, b):
    return lax.dot_general(a, b, (((1,), (0,)), ((), ())), preferred_element_type=jnp.float32)


def flip_rows(value, bit):
    rows, lanes = value.shape
    step = 1 << bit
    if step >= 8:
        parts = [value[at : at + step] for at in range(0, rows, step)]
        return jnp.concatenate([parts[i ^ 1] for i in range(len(parts))], axis=0)
    tiles = value.reshape(rows // 8, 8, lanes)
    up = pltpu.roll(tiles, step, 1)
    if step == 4:
        return up.reshape(rows, lanes)
    down = pltpu.roll(tiles, 8 - step, 1)
    place = lax.broadcasted_iota(jnp.int32, tiles.shape, 1)
    return jnp.where((place // step) % 2 == 1, up, down).reshape(rows, lanes)


def flip_scalar(value, mask, bits):
    for bit in range(bits):
        if mask >> bit & 1:
            step = 1 << bit
            value = value + step - 2 * step * ((value // step) % 2)
    return value


def slot_masks(slot, src_bits, tgt_bits):
    src_mask = sum((slot >> (src_bits - 1 - bit) & 1) << bit for bit in range(src_bits))
    return src_mask, slot >> src_bits


def fused_kernel(
    dims, sig_hbm, leaf_hbm, root_hbm, trans_hbm, slist, tlist, out,
    send_buf, recv_in, recv_out, held, table_a, table_b, weights, root_w, sig, leaf, root, trans,
    send_in_sem, recv_in_sem, send_out_sem, recv_out_sem, load_sem,
):
    n_src, n_tgt, blocks, rank, width, levels, types, degree = dims
    count = n_src * n_tgt
    src_bits = n_src.bit_length() - 1
    tgt_bits = n_tgt.bit_length() - 1
    half = levels // 2
    group = 256 // count
    chunks = blocks // group
    tables = (table_a, table_b)
    s = lax.axis_index("src")
    t = lax.axis_index("tgt")
    me = s * n_tgt + t

    loads = [
        pltpu.make_async_copy(source, target, load_sem.at[i])
        for i, (source, target) in enumerate(
            ((sig_hbm, sig), (leaf_hbm, leaf), (trans_hbm, trans), (root_hbm, root))
        )
    ]
    for load in loads:
        load.start()

    peers = []
    for slot in range(1, count):
        src_mask, tgt_mask = slot_masks(slot, src_bits, tgt_bits)
        peers.append((slot, flip_scalar(s, src_mask, src_bits), flip_scalar(t, tgt_mask, tgt_bits)))
    barrier = pltpu.get_barrier_semaphore()
    for slot, ps, pt in peers:
        pl.semaphore_signal(barrier, inc=1, device_id=(ps, pt), device_id_type=MESH)

    def spread_rows(ref, k, value):
        for tile in range(count // 8):
            ref[pl.ds(tile * 8 * blocks + k, 8, stride=blocks), :] = value[tile * 8 : tile * 8 + 8]

    def gather_rows(ref, k):
        return jnp.concatenate(
            [ref[pl.ds(tile * 8 * blocks + k, 8, stride=blocks), :] for tile in range(count // 8)],
            axis=0,
        )

    def wait_bytes(ref, rows, sem):
        part = ref.at[pl.ds(0, rows)]
        pltpu.make_async_copy(part, part, sem).wait()

    loads[0].wait()
    loads[1].wait()
    for chunk in range(chunks):
        for k in range(chunk * group, (chunk + 1) * group):
            high, low = split(sig[:, k * width : (k + 1) * width])
            map_high, map_low = split(leaf[k])
            y = dot_nt(
                jnp.concatenate([high, low, high], axis=1),
                jnp.concatenate([map_high, map_high, map_low], axis=1),
            )
            spread_rows(send_buf, k, jnp.concatenate([y[:count], y[count:]], axis=1))
        if chunk == 0:
            pl.semaphore_wait(barrier, count - 1)
        for slot, ps, pt in reversed(peers):
            copy = pltpu.make_async_remote_copy(
                src_ref=send_buf.at[pl.ds((ps * n_tgt + pt) * blocks + chunk * group, group)],
                dst_ref=recv_in.at[pl.ds(slot * blocks + chunk * group, group)],
                send_sem=send_in_sem.at[0],
                recv_sem=recv_in_sem.at[chunk],
                device_id=(ps, pt),
                device_id_type=MESH,
            )
            copy.start()
    recv_in[0:blocks, :] = send_buf[pl.ds(me * blocks, blocks), :]

    loads[2].wait()

    def weight_step(level, carry):
        for kind in range(types):
            op = trans[level, kind]
            both = jnp.concatenate([op, op], axis=0).T
            first = lax.broadcasted_iota(jnp.int32, both.shape, 1) < rank
            pair = jnp.concatenate([jnp.where(first, both, 0.0), jnp.where(first, 0.0, both)], axis=0)
            high, low = split(pair)
            lanes = pl.ds(kind * 2 * rank, 2 * rank)
            weights[level, 0 : 2 * rank, lanes] = high
            weights[level, 2 * rank : 4 * rank, lanes] = high
            weights[level, 4 * rank : 6 * rank, lanes] = low
        return carry

    lax.fori_loop(0, levels, weight_step, 0)
    loads[3].wait()

    def root_step(k, carry):
        high, low = split(root[k])
        root_w[k, 0:rank, :] = high
        root_w[k, rank : 2 * rank, :] = high
        root_w[k, 2 * rank : 3 * rank, :] = low
        return carry

    lax.fori_loop(0, blocks, root_step, 0)

    def put(k, value):
        high, low = split(value)
        rows = slice(k * count, (k + 1) * count)
        held[rows, 0 : 2 * rank] = high
        held[rows, 2 * rank : 4 * rank] = low
        held[rows, 4 * rank : 6 * rank] = high

    def multiply(level, chunk):
        rows = held[chunk * group * count : (chunk + 1) * group * count, :]
        for pair in range(types // 2):
            z = dot_nn(rows, weights[level, :, pair * 4 * rank : (pair + 1) * 4 * rank])
            for side in range(2):
                tables[level % 2][2 * pair + side, chunk * group : (chunk + 1) * group] = z[
                    :, side * 2 * rank : (side + 1) * 2 * rank
                ].reshape(group, count, 2 * rank)

    def add_up(level, k):
        if level < half:
            bit = src_bits - 1 - level % src_bits
        else:
            bit = src_bits + (level - half) % tgt_bits
        table = tables[level % 2]
        own = other = None
        for e in range(degree):
            source = slist[level, e, k]
            if e < degree // 2:
                part = table[tlist[level, e, k], source]
                own = part if own is None else own + part
            else:
                part = table[tlist[level, e, k], jnp.maximum(source - blocks, 0)]
                other = part if other is None else other + part
        return own + flip_rows(other, bit)

    for chunk in range(chunks):
        wait_bytes(recv_in, (count - 1) * group, recv_in_sem.at[chunk])
        for k in range(chunk * group, (chunk + 1) * group):
            put(k, gather_rows(recv_in, k))
        multiply(0, chunk)
    wait_bytes(send_buf, (count - 1) * blocks, send_in_sem.at[0])

    for level in range(levels - 1):
        for chunk in range(chunks):
            for k in range(chunk * group, (chunk + 1) * group):
                put(k, add_up(level, k))
            multiply(level + 1, chunk)

    for chunk in range(chunks):
        for k in range(chunk * group, (chunk + 1) * group):
            spread_rows(send_buf, k, add_up(levels - 1, k))
        for slot, ps, pt in reversed(peers):
            copy = pltpu.make_async_remote_copy(
                src_ref=send_buf.at[pl.ds(slot * blocks + chunk * group, group)],
                dst_ref=recv_out.at[pl.ds(me * blocks + chunk * group, group)],
                send_sem=send_out_sem.at[0],
                recv_sem=recv_out_sem.at[chunk],
                device_id=(ps, pt),
                device_id_type=MESH,
            )
            copy.start()
    recv_out[pl.ds(me * blocks, blocks), :] = send_buf[0:blocks, :]

    for chunk in range(chunks):
        wait_bytes(recv_out, (count - 1) * group, recv_out_sem.at[chunk])
        for k in range(chunk * group, (chunk + 1) * group):
            pair = gather_rows(recv_out, k)
            high, low = split(jnp.concatenate([pair[:, :rank], pair[:, rank:]], axis=0))
            y = dot_nn(jnp.concatenate([high, low, high], axis=1), root_w[k])
            out[:, k * width : (k + 1) * width] = y
    wait_bytes(send_buf, (count - 1) * blocks, send_out_sem.at[0])


def local_fused(n_src, n_tgt, signals, leaf_maps, root_maps, translations, source_list, type_list):
    blocks, rank, width = leaf_maps.shape
    levels, types = translations.shape[:2]
    degree = source_list.shape[2]
    count = n_src * n_tgt
    dims = (n_src, n_tgt, blocks, rank, width, levels, types, degree)
    vmem = pl.BlockSpec(memory_space=pltpu.VMEM)
    smem = pl.BlockSpec(memory_space=pltpu.SMEM)
    hbm = pl.BlockSpec(memory_space=pl.ANY)
    lanes = 2 * rank
    chunks = blocks // (256 // count)
    return pl.pallas_call(
        functools.partial(fused_kernel, dims),
        out_shape=jax.ShapeDtypeStruct(signals.shape, jnp.float32),
        in_specs=[hbm, hbm, hbm, hbm, smem, smem],
        out_specs=vmem,
        scratch_shapes=[
            pltpu.VMEM((count * blocks, lanes), jnp.float32),
            pltpu.VMEM((count * blocks, lanes), jnp.float32),
            pltpu.VMEM((count * blocks, lanes), jnp.float32),
            pltpu.VMEM((blocks * count, 3 * lanes), jnp.bfloat16),
            pltpu.VMEM((types, blocks, count, lanes), jnp.float32),
            pltpu.VMEM((types, blocks, count, lanes), jnp.float32),
            pltpu.VMEM((levels, 3 * lanes, types * lanes), jnp.bfloat16),
            pltpu.VMEM((blocks, 3 * rank, width), jnp.bfloat16),
            pltpu.VMEM(signals.shape, jnp.float32),
            pltpu.VMEM(leaf_maps.shape, jnp.float32),
            pltpu.VMEM((blocks, rank, width), jnp.float32),
            pltpu.VMEM(translations.shape, jnp.float32),
            pltpu.SemaphoreType.DMA((1,)),
            pltpu.SemaphoreType.DMA((chunks,)),
            pltpu.SemaphoreType.DMA((1,)),
            pltpu.SemaphoreType.DMA((chunks,)),
            pltpu.SemaphoreType.DMA((4,)),
        ],
        compiler_params=pltpu.CompilerParams(
            collective_id=0, has_side_effects=True, vmem_limit_bytes=58 * 1024 * 1024
        ),
        cost_estimate=pl.CostEstimate(flops=10**9, bytes_accessed=5 * 10**6, transcendentals=0),
    )(
        signals,
        leaf_maps,
        jnp.swapaxes(root_maps, 1, 2),
        translations,
        jnp.swapaxes(source_list, 1, 2),
        jnp.swapaxes(type_list, 1, 2),
    )


def is_power(value):
    return value > 1 and value & (value - 1) == 0


def solution(mesh):
    placed = (
        P(None, ("src", "tgt")),
        P(("src", "tgt"), None, None),
        P(("src", "tgt"), None, None),
        P(),
        P(),
        P(),
    )
    n_src, n_tgt = mesh.shape["src"], mesh.shape["tgt"]

    def local(signals, leaf_maps, *rest):
        blocks, rank, width = leaf_maps.shape
        fits = (
            signals.shape[0] == 2 * n_src * n_tgt
            and is_power(n_src)
            and is_power(n_tgt)
            and 256 % (n_src * n_tgt) == 0
            and blocks % 8 == 0
            and blocks % (256 // (n_src * n_tgt)) == 0
            and rank == 64
            and width == 128
        )
        if fits:
            return local_fused(n_src, n_tgt, signals, leaf_maps, *rest)
        return local_by_axis(signals, leaf_maps, *rest)

    return jax.shard_map(
        local, mesh=mesh, in_specs=placed, out_specs=P(None, ("src", "tgt")), check_vma=False
    )
```
